32 devices in a mesh: seq: 8 (over z, y), tp: 4 (over x, core).
Axes of the slice: x: 2, y: 2, z: 4, core: 2. Of those that a mesh axis runs over, the one named last changes fastest.
Arguments:
- residual: bfloat16 [2048, 3584], P(('seq', 'tp')), may hold values from -6 to 6
- x_in: bfloat16 [2048, 3584], P('seq', 'tp'), may hold values from -6 to 6
- z_in: bfloat16 [2048, 3584], P('seq', 'tp'), may hold values from -6 to 6
- bc_in: bfloat16 [2048, 128], P('seq'), may hold values from -1.5 to 1.5
- dt_in: float32 [2048, 56], P('seq', 'tp'), may hold values from -6 to 6
- conv_x_weight: float32 [4, 3584], P(None, 'tp'), may hold values from -3 to 3
- conv_bc_weight: float32 [4, 128], replicated, may hold values from -3 to 3
- conv_x_cache: bfloat16 [4, 3, 3584], P(None, None, 'tp'), may hold values from -6 to 6
- conv_bc_cache: bfloat16 [4, 3, 128], replicated, may hold values from -1.5 to 1.5
- ssm_cache: float32 [4, 56, 64, 64], P(None, 'tp'), may hold values from -12 to 12
- dt_bias: float32 [56], P('tp'), may hold values from -1 to 1
- a_log: float32 [56], P('tp'), may hold values from -9 to -3.5
- d_skip: float32 [56], P('tp'), may hold values from 0.5 to 1.5
- norm_gain: float32 [3584], P('tp'), may hold values from 0.5 to 1.5
- out_weight: bfloat16 [3584, 3584], P('tp'), may hold values from -0.09375 to 0.09375
- attn_gain: float32 [3584], replicated, may hold values from 0.5 to 1.5
- q_weight: bfloat16 [3584, 3584], P(None, 'tp'), may hold values from -1 to 1
- q_down: bfloat16 [3584, 128], replicated, may hold values from -0.09375 to 0.09375
- q_up: bfloat16 [128, 3584], P(None, 'tp'), may hold values from -0.5 to 0.5
- cache_keys: bfloat16 [2048, 3584], P('seq', 'tp'), may hold values from -6 to 6
- cache_values: bfloat16 [2048, 3584], P('seq', 'tp'), may hold values from -6 to 6
- new_keys: bfloat16 [2048, 3584], P('seq', 'tp'), may hold values from -6 to 6
- new_values: bfloat16 [2048, 3584], P('seq', 'tp'), may hold values from -6 to 6
- lengths: int32 [4], replicated, may hold values from 1 to 768, 2048 in all
Outputs:
- hidden: bfloat16 [2048, 3584], P(('seq', 'tp'))
- attended: bfloat16 [2048, 3584], P('seq', 'tp')
The draws below stay inside these ranges and needn't reach their ends.
Inputs may be any that keep to these rules, and one draw needn't show every extreme that they name: lengths of the prompts' second halves sum to 2048; the largest is 768.
All inputs are finite; a program needn't handle non-finite values.
Results may differ from the reference program's by a relative error of at most 0.014.
Values may be sent and summed in bfloat16 or wider, within the bound.
A program may use at most 192 MiB of HBM per device.

```python
import math
import jax
import jax.numpy as jnp
import numpy as np
from jax import lax

D = 3584
MH = 56
HD = 64
N = 64
KW = 4
INNER = 3584
AH = 16
HA = 224
QW = 3584
RANK = 128
TOK_DEV = 256
REACH = 3
HALF_MAX = 768
TOKENS = 2048
PROMPTS = 4


def draw_residual(key, part):
    noise = jax.random.normal(jax.random.fold_in(key, 7002), (TOKENS, D), jnp.float32)
    values = noise
    return jnp.clip(values, -6.0, 6.0).astype(jnp.bfloat16)


def draw_q_weight(key, part):
    noise = jnp.clip(jax.random.normal(jax.random.fold_in(key, 7003), (D, QW), jnp.float32), -6.0, 6.0) / D ** 0.5
    values = noise
    return jnp.clip(values, -1.0, 1.0).astype(jnp.bfloat16)


def draw_cache_keys(key, part):
    noise = jnp.clip(jax.random.normal(jax.random.fold_in(key, 7004), (TOKENS, QW), jnp.float32), -6.0, 6.0)
    values = noise
    return values.astype(jnp.bfloat16)


def shard_levels(key, shape, cuts, least, high):
    level = 1.0
    for dim, shards_of in cuts:
        heights = jax.random.uniform(jax.random.fold_in(jax.random.fold_in(key, 6), dim), (shards_of,), jnp.float32, least / len(cuts), high / len(cuts))
        level = level * jnp.repeat(jnp.exp(heights), shape[dim] // shards_of).reshape((-1,) + (1,) * (len(shape) - 1 - dim))
    return level


def split_up(amount, total, most, skew):
    weights = [(1 << 20) // math.isqrt(standing ** skew) + 1 for standing in range(2, amount + 1)]
    surplus, holding = total - most - (amount - 1), [1] * (amount - 1)
    while surplus > 0:
        free = [i for i in range(amount - 1) if holding[i] < most]
        mass, left = sum([weights[i] for i in free]), surplus
        for i in free:
            extra = min(most - holding[i], max(1, left * weights[i] // mass), surplus)
            holding[i] = holding[i] + extra
            surplus = surplus - extra
    return np.array([most] + holding)


def ragged_sizes(key, amount, total, bound, skew):
    if amount == 2:
        one = jax.random.randint(key, (), max(1, total - bound), min(bound, total - 1) + 1)
        return jnp.stack([one, total - one])
    sizes = jnp.asarray(split_up(amount, total, bound, skew), jnp.int32)
    twos = (amount - 1) // 2
    source_of, taker = sizes[1:1 + 2 * twos:2], sizes[2:2 + 2 * twos:2]
    slack = jnp.minimum(source_of - 1, bound - taker)
    moved = jax.random.randint(jax.random.fold_in(key, 1), (twos,), 0, 1 << 20) % (slack + 1)
    sizes = sizes.at[1:1 + 2 * twos:2].set(source_of - moved).at[2:2 + 2 * twos:2].set(taker + moved)
    return sizes[jax.random.permutation(jax.random.fold_in(key, 2), amount)]


def bell_draw(key, dims, scale, most, cuts=(), held_as=jnp.bfloat16):
    loudness = shard_levels(key, dims, cuts, -0.22, 0.18) if cuts else 1.0
    drawn = jax.random.normal(key, dims, jnp.float32) * scale * loudness
    return jnp.minimum(jnp.maximum(drawn, -most), most).astype(held_as)


def setup_inputs(seed: int = 0) -> dict:
    key_of = jax.random.split(jax.random.key(seed), 25)
    residual = draw_residual(jax.random.fold_in(key_of[24], 71), 0)
    x_in = bell_draw(key_of[1], (TOKENS, INNER), 1.0, 6.0, ((0, 8), (1, 4)))
    z_in = bell_draw(key_of[2], (TOKENS, INNER), 1.0, 6.0, ((0, 8), (1, 4)))
    bc_in = bell_draw(key_of[3], (TOKENS, 2 * N), 0.25, 1.5, ((0, 8),))
    dt_in = bell_draw(key_of[4], (TOKENS, MH), 1.0, 6.0, ((0, 8), (1, 4)), jnp.float32)
    conv_x_weight = bell_draw(key_of[5], (KW, INNER), 0.5, 3.0, ((1, 4),), jnp.float32)
    conv_bc_weight = bell_draw(key_of[6], (KW, 2 * N), 0.5, 3.0, (), jnp.float32)
    conv_x_cache = bell_draw(key_of[7], (PROMPTS, KW - 1, INNER), 1.0, 6.0, ((2, 4),))
    conv_bc_cache = bell_draw(key_of[8], (PROMPTS, KW - 1, 2 * N), 0.25, 1.5)
    ssm_cache = bell_draw(key_of[9], (PROMPTS, MH, HD, N), 2.0, 12.0, ((1, 4),), jnp.float32)
    dt_bias = jnp.clip(jax.random.uniform(key_of[10], (MH,), jnp.float32, -1.0, 1.0) * shard_levels(key_of[10], (MH,), ((0, 4),), -0.4, 0.0), -1.0, 1.0)
    a_log = jnp.clip(-9.0 + 5.5 * jax.random.uniform(key_of[11], (MH,), jnp.float32) ** shard_levels(key_of[11], (MH,), ((0, 4),), -0.2, 0.2), -9.0, -3.5)
    d_skip = jnp.clip(0.5 + 1.0 * jax.random.uniform(key_of[12], (MH,), jnp.float32) ** shard_levels(key_of[12], (MH,), ((0, 4),), -0.2, 0.2), 0.5, 1.5)
    norm_gain = jnp.clip(1.0 + 0.1 * jax.random.normal(key_of[13], (INNER,), jnp.float32), 0.5, 1.5)
    out_weight = bell_draw(key_of[14], (INNER, D), INNER ** -0.5, 0.09375, ((0, 4),))
    attn_gain = jnp.clip(1.0 + 0.1 * jax.random.normal(key_of[15], (D,), jnp.float32), 0.5, 1.5)
    q_weight = draw_q_weight(jax.random.fold_in(key_of[24], 71), 0)
    q_down = bell_draw(key_of[17], (D, RANK), D ** -0.5, 0.09375)
    q_up = bell_draw(key_of[18], (RANK, QW), RANK ** -0.5, 0.5, ((1, 4),))
    cache_keys = draw_cache_keys(jax.random.fold_in(key_of[24], 71), 0)
    cache_values = bell_draw(key_of[20], (TOKENS, QW), 1.0, 6.0, ((0, 8), (1, 4)))
    new_keys = bell_draw(key_of[21], (TOKENS, QW), 1.0, 6.0, ((0, 8), (1, 4)))
    new_values = bell_draw(key_of[22], (TOKENS, QW), 1.0, 6.0, ((0, 8), (1, 4)))
    lengths = ragged_sizes(key_of[23], PROMPTS, TOKENS, HALF_MAX, 2).astype(jnp.int32)
    return {"residual": residual, "x_in": x_in, "z_in": z_in, "bc_in": bc_in, "dt_in": dt_in, "conv_x_weight": conv_x_weight, "conv_bc_weight": conv_bc_weight, "conv_x_cache": conv_x_cache, "conv_bc_cache": conv_bc_cache, "ssm_cache": ssm_cache, "dt_bias": dt_bias, "a_log": a_log, "d_skip": d_skip, "norm_gain": norm_gain, "out_weight": out_weight, "attn_gain": attn_gain, "q_weight": q_weight, "q_down": q_down, "q_up": q_up, "cache_keys": cache_keys, "cache_values": cache_values, "new_keys": new_keys, "new_values": new_values, "lengths": lengths}


EPS = 1e-05
NEG = -1e+30

def locate(lengths, index):
    ends = jnp.cumsum(lengths).astype(jnp.int32)
    starts = (ends - lengths).astype(jnp.int32)
    count = lengths.shape[0]
    segment = lax.optimization_barrier(jnp.sum((index[:, None] >= ends[None, :]).astype(jnp.int32), axis=1)).astype(jnp.int32)
    segment = jnp.minimum(segment, count - 1)
    onehot = segment[:, None] == jnp.arange(count, dtype=jnp.int32)[None, :]
    begin = lax.optimization_barrier(jnp.sum(jnp.where(onehot, starts[None, :], 0), axis=1)).astype(jnp.int32)
    valid = (index >= 0) & (index < ends[count - 1])
    return (segment, begin, valid, onehot)

def convolve(inputs, cache, weight, position, onehot):
    taps = weight.shape[0]
    length = inputs.shape[0]
    padded = jnp.concatenate([jnp.zeros((taps - 1, inputs.shape[1]), inputs.dtype), inputs], axis=0)
    picks = onehot.astype(jnp.float32)
    cached_rows = [jnp.dot(picks, cache[:, slot, :].astype(jnp.float32), precision=lax.Precision.HIGHEST) for slot in range(taps - 1)]
    result = weight[0][None, :] * inputs.astype(jnp.float32)
    for lag in range(1, taps):
        shifted = padded[taps - 1 - lag:taps - 1 - lag + length].astype(jnp.float32)
        slot_index = taps - 1 + position - lag
        fallback = jnp.zeros_like(shifted)
        for slot in range(taps - 1):
            fallback = jnp.where((slot_index == slot)[:, None], cached_rows[slot], fallback)
        shifted = jnp.where((position >= lag)[:, None], shifted, fallback)
        result = result + weight[lag][None, :] * shifted
    return jax.nn.silu(result).astype(jnp.bfloat16)

def reference(residual, x_in, z_in, bc_in, dt_in, conv_x_weight, conv_bc_weight, conv_x_cache, conv_bc_cache, ssm_cache, dt_bias, a_log, d_skip, norm_gain, out_weight, attn_gain, q_weight, q_down, q_up, cache_keys, cache_values, new_keys, new_values, lengths):
    index = jnp.arange(TOKENS, dtype=jnp.int32)
    segment, begin, valid, onehot = locate(lengths, index)
    position = (index - begin).astype(jnp.int32)
    x_conv = convolve(x_in, conv_x_cache, conv_x_weight, position, onehot)
    bc_conv = convolve(bc_in, conv_bc_cache, conv_bc_weight, position, onehot)
    values = x_conv.astype(jnp.float32).reshape(TOKENS, MH, HD)
    inputs_b = bc_conv[:, :N].astype(jnp.float32)
    inputs_c = bc_conv[:, N:].astype(jnp.float32)
    step = jax.nn.softplus(dt_in + dt_bias[None, :])
    decay = jnp.exp(-step * jnp.exp(a_log)[None, :])

    def advance(state, inputs):
        x_row, b_row, c_row, decay_row, step_row, start_row, segment_row = inputs
        cached = lax.dynamic_index_in_dim(ssm_cache, segment_row, 0, keepdims=False)
        state = jnp.where(start_row, cached, state)
        state = decay_row[:, None, None] * state + (step_row[:, None] * x_row)[:, :, None] * b_row[None, None, :]
        return (state, lax.optimization_barrier(jnp.sum(state * c_row[None, None, :], axis=2)))
    initial = jnp.zeros((MH, HD, N), jnp.float32)
    _, outputs = lax.scan(advance, initial, (values, inputs_b, inputs_c, decay, step, position == 0, segment))
    mixed = outputs + d_skip[None, :, None] * values
    gated = (mixed * jax.nn.silu(z_in.astype(jnp.float32).reshape(TOKENS, MH, HD))).reshape(TOKENS, INNER)
    normed = (gated * lax.rsqrt(lax.optimization_barrier(jnp.mean(gated * gated, axis=1, keepdims=True)) + EPS) * norm_gain[None, :]).astype(jnp.bfloat16)
    hidden = (residual.astype(jnp.float32) + jnp.dot(normed, out_weight, preferred_element_type=jnp.float32)).astype(jnp.bfloat16)
    level = hidden.astype(jnp.float32)
    attn_in = (level * lax.rsqrt(lax.optimization_barrier(jnp.mean(level * level, axis=1, keepdims=True)) + EPS) * attn_gain[None, :]).astype(jnp.bfloat16)
    low = jnp.dot(attn_in, q_down, preferred_element_type=jnp.float32).astype(jnp.bfloat16)
    query = (jnp.dot(attn_in, q_weight, preferred_element_type=jnp.float32) + jnp.dot(low, q_up, preferred_element_type=jnp.float32)).astype(jnp.bfloat16)
    span = REACH * TOK_DEV
    padding = ((span, span), (0, 0))
    padded_ck = jnp.pad(cache_keys, padding)
    padded_cv = jnp.pad(cache_values, padding)
    padded_nk = jnp.pad(new_keys, padding)
    padded_nv = jnp.pad(new_values, padding)
    cache_span = (2 * REACH + 1) * TOK_DEV
    new_span = (REACH + 1) * TOK_DEV
    scale = 1.0 / HA ** 0.5

    def block_out(block_index):
        start = (block_index * TOK_DEV).astype(jnp.int32)
        query_index = start + jnp.arange(TOK_DEV, dtype=jnp.int32)
        query_segment = lax.dynamic_slice_in_dim(segment, start, TOK_DEV, 0)
        rows = lax.dynamic_slice_in_dim(query, start, TOK_DEV, 0).astype(jnp.float32).reshape(TOK_DEV, AH, HA)
        cache_index = (start - span + jnp.arange(cache_span, dtype=jnp.int32)).astype(jnp.int32)
        new_index = (start - span + jnp.arange(new_span, dtype=jnp.int32)).astype(jnp.int32)
        cache_segment, _, cache_valid, _ = locate(lengths, cache_index)
        new_segment, _, new_valid, _ = locate(lengths, new_index)
        cache_mask = cache_valid[None, :] & (cache_segment[None, :] == query_segment[:, None])
        new_mask = new_valid[None, :] & (new_segment[None, :] == query_segment[:, None]) & (new_index[None, :] <= query_index[:, None])
        mask = jnp.concatenate([cache_mask, new_mask], axis=1)
        keys = jnp.concatenate([lax.dynamic_slice_in_dim(padded_ck, start, cache_span, 0), lax.dynamic_slice_in_dim(padded_nk, start, new_span, 0)], axis=0)
        vals = jnp.concatenate([lax.dynamic_slice_in_dim(padded_cv, start, cache_span, 0), lax.dynamic_slice_in_dim(padded_nv, start, new_span, 0)], axis=0)
        keys = keys.astype(jnp.float32).reshape(-1, AH, HA)
        vals = vals.astype(jnp.float32).reshape(-1, AH, HA)
        scores = jnp.einsum('qhd,khd->hqk', rows, keys) * scale
        scores = jnp.where(mask[None], scores, NEG)
        top = lax.optimization_barrier(jnp.max(scores, axis=2, keepdims=True))
        weights = jnp.exp(scores - top)
        probs = (weights / lax.optimization_barrier(jnp.sum(weights, axis=2, keepdims=True))).astype(jnp.bfloat16)
        result = jnp.einsum('hqk,khd->qhd', probs.astype(jnp.float32), vals)
        return result.reshape(TOK_DEV, QW).astype(jnp.bfloat16)
    blocks = lax.map(block_out, jnp.arange(TOKENS // TOK_DEV, dtype=jnp.int32))
    attended = blocks.reshape(TOKENS, QW)
    return (hidden, attended)
```

```python
import functools

import jax
import jax.numpy as jnp
from jax import lax
from jax.experimental import pallas as pl
from jax.experimental.pallas import tpu as pltpu
from jax.sharding import PartitionSpec as P

HA = 224


EPS = 1e-05
NEG = -1e30


def shifted_2(value, axis, steps):
    count = lax.axis_size(axis)
    initial, last = (max(0, -steps), min(count, count - steps))
    pairs = [(source, source + steps) for source in range(initial, last)]
    return jax.tree.map(lambda a: lax.ppermute(a, axis, pairs), value)


def prefix(part, axis, combine, reach):
    hops = [shifted_2(part, axis, distance) for distance in range(1, reach + 1)]
    state = hops[reach - 1]
    for distance in range(reach - 1, 0, -1):
        state = combine(state, hops[distance - 1])
    return state


def project_kernel(
    g_ref, sq_ref, res_ref, gain_ref, up_ref, ow_hbm, qw_hbm, qd_hbm,
    hid_ref, query_ref,
    ow, qw, qd, part, send1, recv1, send2, recv2, sq_recv, total, gathered, acc, low_acc,
    w_sem, s1, r1, s2, r2, s3, r3, s4, r4, s5, r5, s6, r6,
):
    me = lax.axis_index("tp")
    core, x = lax.rem(me, 2), me // 2
    mate = x * 2 + (1 - core)
    across = (1 - x) * 2 + core
    corner = (1 - x) * 2 + (1 - core)
    share = res_ref.shape[0]
    chunks, width = send2.shape[0], send2.shape[2]
    copies = [
        pltpu.make_async_copy(ow_hbm, ow, w_sem.at[0]),
        pltpu.make_async_copy(qw_hbm, qw, w_sem.at[1]),
        pltpu.make_async_copy(qd_hbm, qd, w_sem.at[2]),
    ]
    for copy in copies:
        copy.start()

    barrier = pltpu.get_barrier_semaphore()
    for other in (mate, across, corner):
        pl.semaphore_signal(
            barrier, inc=1, device_id={"tp": other}, device_id_type=pl.DeviceIdType.MESH
        )
    pl.semaphore_wait(barrier, 3)

    def rows(owner):
        return pl.ds(pl.multiple_of(owner * share, share), share)

    def remote(src, dst, send, recv, other):
        return pltpu.make_async_remote_copy(
            src_ref=src,
            dst_ref=dst,
            send_sem=send,
            recv_sem=recv,
            device_id={"tp": other},
            device_id_type=pl.DeviceIdType.MESH,
        )

    sq_copies = [
        remote(sq_ref.at[rows(other)], sq_recv.at[k], s3.at[k], r3.at[k], other)
        for k, other in enumerate((mate, across, corner))
    ]
    for copy in sq_copies:
        copy.start()
    copies[0].wait()

    def first(i):
        return remote(send1.at[i], recv1.at[i], s1.at[i], r1.at[i], mate)

    def second(i):
        return remote(send2.at[i], recv2.at[i], s2.at[i], r2.at[i], across)

    def columns(i):
        return pl.ds(pl.multiple_of(i * width, width), width)

    @pl.loop(0, chunks)
    def _(i):
        cols = columns(i)
        part[:, cols] = jnp.dot(g_ref[...], ow[:, cols], preferred_element_type=jnp.float32)
        for half in range(2):
            send1[i, half] = part[rows(half * 2 + (1 - core)), cols].astype(jnp.bfloat16)
        first(i).start()

    @pl.loop(0, chunks)
    def _(i):
        first(i).wait()
        cols = columns(i)
        send2[i] = (
            part[rows(across), cols] + recv1[i, 1 - x].astype(jnp.float32)
        ).astype(jnp.bfloat16)
        second(i).start()

    for copy in sq_copies:
        copy.wait()
    squares = sq_ref[rows(me)] + sq_recv[0] + sq_recv[1] + sq_recv[2]
    inner = g_ref.shape[1] * 4
    ratio = lax.rsqrt(squares[:, :1] / inner + EPS)

    @pl.loop(0, chunks)
    def _(i):
        second(i).wait()
        cols = columns(i)
        summed = (
            part[rows(me), cols]
            + recv1[i, x].astype(jnp.float32)
            + recv2[i].astype(jnp.float32)
        )
        hidden = (res_ref[:, cols].astype(jnp.float32) + ratio * summed).astype(jnp.bfloat16)
        hid_ref[:, cols] = hidden
        level = hidden.astype(jnp.float32)
        square = jnp.sum(level * level, axis=1, keepdims=True)
        total[...] = jnp.where(i == 0, square, total[...] + square)

    features = res_ref.shape[1]
    scale = lax.rsqrt(total[:, :1] / features + EPS)

    def over(i):
        place = (me, slice(None), columns(i))
        return remote(gathered.at[place], gathered.at[place], s4.at[i], r4.at[i], across)

    def beside(i):
        place = (me, slice(None), columns(i))
        return remote(gathered.at[place], gathered.at[place], s5.at[i], r5.at[i], mate)

    def onward(i):
        place = (across, slice(None), columns(i))
        return remote(gathered.at[place], gathered.at[place], s6.at[i], r6.at[i], mate)

    @pl.loop(0, chunks)
    def _(i):
        cols = columns(i)
        gathered[me, :, cols] = (
            hid_ref[:, cols].astype(jnp.float32) * scale * gain_ref[:, cols]
        ).astype(jnp.bfloat16)
        over(i).start()
        beside(i).start()

    @pl.loop(0, chunks)
    def _(i):
        over(i).wait_recv()
        onward(i).start()

    copies[1].wait()
    copies[2].wait()

    @pl.loop(0, chunks)
    def _(i):
        over(i).wait_send()
        beside(i).wait()
        onward(i).wait()
        cols = columns(i)
        block = gathered[:, :, cols].reshape(4 * share, width)
        product = jnp.dot(block, qw[cols, :], preferred_element_type=jnp.float32)
        adapted = jnp.dot(block, qd[cols, :], preferred_element_type=jnp.float32)
        acc[...] = jnp.where(i == 0, product, acc[...] + product)
        low_acc[...] = jnp.where(i == 0, adapted, low_acc[...] + adapted)

    low = low_acc[...].astype(jnp.bfloat16)
    query_ref[...] = (
        acc[...] + jnp.dot(low, up_ref[...], preferred_element_type=jnp.float32)
    ).astype(jnp.bfloat16)


def project(g, squares, residual, attn_gain, q_up, out_weight, q_weight, q_down):
    share, features = residual.shape
    length, inner = g.shape
    columns, rank = q_weight.shape[1], q_down.shape[1]
    width = 512
    chunks = features // width
    bf, f32 = jnp.bfloat16, jnp.float32
    vmem = pl.BlockSpec(memory_space=pltpu.VMEM)
    hbm = pl.BlockSpec(memory_space=pl.ANY)
    dma = pltpu.SemaphoreType.DMA
    return pl.pallas_call(
        project_kernel,
        out_shape=(
            jax.ShapeDtypeStruct((share, features), bf),
            jax.ShapeDtypeStruct((length, columns), bf),
        ),
        in_specs=[vmem] * 5 + [hbm] * 3,
        out_specs=(vmem, vmem),
        scratch_shapes=[
            pltpu.VMEM(out_weight.shape, bf),
            pltpu.VMEM(q_weight.shape, bf),
            pltpu.VMEM(q_down.shape, bf),
            pltpu.VMEM((length, features), f32),
            pltpu.VMEM((chunks, 2, share, width), bf),
            pltpu.VMEM((chunks, 2, share, width), bf),
            pltpu.VMEM((chunks, share, width), bf),
            pltpu.VMEM((chunks, share, width), bf),
            pltpu.VMEM((3, share, 128), f32),
            pltpu.VMEM((share, 128), f32),
            pltpu.VMEM((4, share, features), bf),
            pltpu.VMEM((length, columns), f32),
            pltpu.VMEM((length, rank), f32),
            dma((3,)),
        ]
        + [dma((chunks,))] * 4
        + [dma((3,))] * 2
        + [dma((chunks,))] * 6,
        compiler_params=pltpu.CompilerParams(
            collective_id=0, has_side_effects=True, vmem_limit_bytes=44 * 2**20
        ),
        cost_estimate=pl.CostEstimate(
            flops=4 * length * inner * features, bytes_accessed=400 * 2**20, transcendentals=0
        ),
        name="project",
    )(g, squares, residual, attn_gain.reshape(1, features), q_up, out_weight, q_weight, q_down)


def attend_kernel(offsets, near_ref, query_ref, begin_ref, end_ref, *refs):
    pieces = refs[: -4]
    out_ref, acc, top_ref, sum_ref = refs[-4:]
    length, width = query_ref.shape
    heads = width // HA
    scale = 1.0 / HA**0.5
    first = near_ref[0]
    low, high = near_ref[1], near_ref[2]
    lanes = lax.broadcasted_iota(jnp.int32, (length, length), 1)
    own = lax.broadcasted_iota(jnp.int32, (length, length), 0)
    windows = []
    for head in range(heads):
        left = head * HA // 128 * 128
        right = -(-(head + 1) * HA // 128) * 128
        windows.append((left, right))
    top_ref[...] = jnp.full_like(top_ref, NEG)
    sum_ref[...] = jnp.zeros_like(sum_ref)
    acc[...] = jnp.zeros_like(acc)

    def member(head):
        left, right = windows[head]
        column = left + lax.broadcasted_iota(jnp.int32, (length, right - left), 1)
        return (column >= head * HA) & (column < (head + 1) * HA)

    def visit(keys, values, offset, causal):
        start = first + offset * length
        index = start + lanes
        mask = (index >= begin_ref[:, :1]) & (index < end_ref[:, :1])
        if causal:
            mask = mask & (index <= first + own)
        for head in range(heads):
            left, right = windows[head]
            query = jnp.where(member(head), query_ref[:, left:right], jnp.bfloat16(0))
            scores = (
                lax.dot_general(
                    query,
                    keys[0][:, keys[1] + left : keys[1] + right],
                    (((1,), (1,)), ((), ())),
                    preferred_element_type=jnp.float32,
                )
                * scale
            )
            scores = jnp.where(mask, scores, NEG)
            old = top_ref[head][:, :1]
            top = jnp.maximum(old, jnp.max(scores, axis=1, keepdims=True))
            weights = jnp.exp(scores - top)
            shrink = jnp.exp(old - top)
            shape = (length, 128)
            top_ref[head] = jnp.broadcast_to(top, shape)
            sum_ref[head] = sum_ref[head] * shrink + jnp.sum(weights, axis=1, keepdims=True)
            acc[head, :, : right - left] = acc[head, :, : right - left] * shrink + jnp.dot(
                weights.astype(jnp.bfloat16),
                values[0][:, values[1] + left : values[1] + right],
                preferred_element_type=jnp.float32,
            )

    def entry(piece, part):
        if piece < 0:
            return (pieces[part], 0)
        return (pieces[4 + piece], part * width)

    for place, (piece, offset, causal) in enumerate(offsets):
        part = 2 if causal else 0
        keys, values = entry(piece, part), entry(piece, part + 1)
        start = first + offset * length
        if offset == 0:
            visit(keys, values, offset, causal)
        else:
            pl.when((start < high) & (start + length > low))(
                functools.partial(visit, keys, values, offset, causal)
            )
    for head in range(heads):
        left, right = windows[head]
        result = acc[head, :, : right - left] / sum_ref[head][:, :1]
        result = result.astype(jnp.bfloat16)
        if head == 0:
            out_ref[:, left:right] = result
        else:
            shared = windows[head - 1][1]
            kept = jnp.where(
                member(head)[:, : shared - left], result[:, : shared - left], out_ref[:, left:shared]
            )
            out_ref[:, left:shared] = kept
            out_ref[:, shared:right] = result[:, shared - left :]


def attend_all(query, begin, end, first, own, behind, forward):
    length, width = query.shape
    heads = width // HA
    offsets = [(-1, 0, False), (-1, 0, True)]
    for place in range(len(behind)):
        offsets += [(place, -place - 1, False), (place, -place - 1, True)]
    for place in range(len(forward)):
        offsets.append((len(behind) + place, place + 1, False))
    low, high = begin[0], end[length - 1]
    near = jnp.stack([first, low, high]).astype(jnp.int32)
    spread = lambda a: jnp.broadcast_to(a[:, None], (length, 128)).astype(jnp.int32)
    vmem = pl.BlockSpec(memory_space=pltpu.VMEM)
    return pl.pallas_call(
        functools.partial(attend_kernel, tuple(offsets)),
        out_shape=jax.ShapeDtypeStruct((length, width), jnp.bfloat16),
        in_specs=[pl.BlockSpec(memory_space=pltpu.SMEM)]
        + [vmem] * (3 + 4 + len(behind) + len(forward)),
        out_specs=vmem,
        scratch_shapes=[
            pltpu.VMEM((heads, length, 384), jnp.float32),
            pltpu.VMEM((heads, length, 128), jnp.float32),
            pltpu.VMEM((heads, length, 128), jnp.float32),
        ],
        compiler_params=pltpu.CompilerParams(vmem_limit_bytes=48 * 2**20),
        name="attend",
    )(near, query, spread(begin), spread(end), *own, *behind, *forward)


def locate(lengths, index):
    ends = jnp.cumsum(lengths)
    starts = ends - lengths
    count = lengths.shape[0]
    segment = jnp.sum((index[:, None] >= ends[None, :]).astype(jnp.int32), axis=1)
    segment = jnp.minimum(segment, count - 1)
    onehot = segment[:, None] == jnp.arange(count, dtype=jnp.int32)[None, :]
    begin = jnp.sum(jnp.where(onehot, starts[None, :], 0), axis=1)
    valid = (index >= 0) & (index < ends[count - 1])
    return (segment, begin, valid, onehot)


def convolve(inputs, border, cache, weight, position, onehot):
    taps = weight.shape[0]
    length = inputs.shape[0]
    extended = jnp.concatenate([border, inputs], axis=0)
    picks = onehot.astype(jnp.bfloat16)
    cached_rows = [
        jnp.dot(picks, cache[:, slot, :], preferred_element_type=jnp.float32)
        for slot in range(taps - 1)
    ]
    result = weight[0][None, :] * inputs.astype(jnp.float32)
    for lag in range(1, taps):
        shifted = extended[taps - 1 - lag : taps - 1 - lag + length].astype(jnp.float32)
        slot_index = taps - 1 + position - lag
        fallback = jnp.zeros_like(shifted)
        for slot in range(taps - 1):
            fallback = jnp.where((slot_index == slot)[:, None], cached_rows[slot], fallback)
        shifted = jnp.where((position >= lag)[:, None], shifted, fallback)
        result = result + weight[lag][None, :] * shifted
    return jax.nn.silu(result).astype(jnp.bfloat16)


def per_device(
    residual,
    x_in,
    z_in,
    bc_in,
    dt_in,
    conv_x_weight,
    conv_bc_weight,
    conv_x_cache,
    conv_bc_cache,
    ssm_cache,
    dt_bias,
    a_log,
    d_skip,
    norm_gain,
    out_weight,
    attn_gain,
    q_weight,
    q_down,
    q_up,
    cache_keys,
    cache_values,
    new_keys,
    new_values,
    lengths,
):
    high_precision = lax.Precision.HIGH
    length = x_in.shape[0]
    taps = conv_x_weight.shape[0]
    seq_index = lax.axis_index("seq")
    seq_count = lax.axis_size("seq")
    reach = seq_count // 4 + 1
    first = seq_index * length
    packed = jnp.concatenate([cache_keys, cache_values, new_keys, new_values], axis=1)
    packed_cache = packed[:, : 2 * cache_keys.shape[1]]
    behind = [shifted_2(packed, "seq", distance) for distance in range(1, reach + 1)]
    forward = [shifted_2(packed_cache, "seq", -distance) for distance in range(1, reach + 1)]
    local_index = first + jnp.arange(length, dtype=jnp.int32)
    segment, begin, valid, onehot = locate(lengths, local_index)
    position = local_index - begin
    x_border, bc_border = shifted_2(
        (x_in[length - taps + 1 :], bc_in[length - taps + 1 :]), "seq", 1
    )
    x_conv = convolve(x_in, x_border, conv_x_cache, conv_x_weight, position, onehot)
    bc_conv = convolve(bc_in, bc_border, conv_bc_cache, conv_bc_weight, position, onehot)
    heads = dt_bias.shape[0]
    state_size = bc_in.shape[1] // 2
    head_size = x_in.shape[1] // heads
    prompts = lengths.shape[0]
    values_bf = x_conv.reshape(length, heads, head_size)
    values = x_conv.astype(jnp.float32).reshape(length, heads, head_size)
    inputs_b = bc_conv[:, :state_size]
    inputs_c = bc_conv[:, state_size:]
    step = jax.nn.softplus(dt_in + dt_bias[None, :])
    log_decay = -step * jnp.exp(a_log)[None, :]
    cumulative = jnp.cumsum(log_decay, axis=0)
    local_begin = jnp.maximum(begin - first, 0)
    before = jnp.take(cumulative - log_decay, local_begin, axis=0)
    from_begin = jnp.exp(cumulative - before)
    block = min(length, 512)
    pair_scores = jnp.dot(inputs_c, inputs_b.T, preferred_element_type=jnp.float32)
    cumulative_t = cumulative.T
    step_t = step.T
    order = jnp.arange(length, dtype=jnp.int32)

    def intra(block_start):
        query_rows = block_start + jnp.arange(block, dtype=jnp.int32)
        same = (segment[:, None] == segment[None, :]) & (query_rows[:, None] >= order[None, :])
        gap = cumulative_t[:, :, None] - cumulative_t[:, None, :]
        factor = jnp.where(same[None], jnp.exp(jnp.where(same[None], gap, 0.0)), 0.0)
        weights = factor * step_t[:, None, :] * pair_scores[None, :, :]
        return jnp.einsum(
            "hqs,shd->qhd",
            weights,
            values_bf,
            precision=high_precision,
            preferred_element_type=jnp.float32,
        )

    intra_out = lax.map(intra, jnp.arange(length // block, dtype=jnp.int32) * block).reshape(
        length, heads, head_size
    )
    last_segment = segment[length - 1]
    in_last = segment == last_segment
    tail_weight = (
        jnp.where(in_last[:, None], jnp.exp(cumulative[length - 1][None, :] - cumulative), 0.0)
        * step
    )
    weighted = tail_weight[:, :, None] * values
    local_state = jnp.einsum(
        "thd,tn->hdn",
        weighted,
        inputs_b,
        precision=high_precision,
        preferred_element_type=jnp.float32,
    )
    whole_decay = jnp.exp(cumulative[length - 1] - before[length - 1])
    starts_here = begin[length - 1] >= first
    cached_last = lax.dynamic_index_in_dim(ssm_cache, last_segment, 0, keepdims=False)
    chain_state = local_state + jnp.where(
        starts_here, whole_decay[:, None, None] * cached_last, 0.0
    )
    chain_decay = jnp.where(starts_here, jnp.zeros_like(whole_decay), whole_decay)

    def combine(earlier, later):
        return (earlier[0] * later[0], later[0][:, None, None] * earlier[1] + later[1])

    carried_decay, carried = prefix((chain_decay, chain_state), "seq", combine, reach)
    continuing = position[0] > 0
    replace = (jnp.arange(prompts, dtype=jnp.int32) == segment[0]) & continuing
    initial = jnp.where(replace[:, None, None, None], carried[None], ssm_cache)
    selected = (onehot[:, :, None].astype(jnp.bfloat16) * inputs_c[:, None, :]).reshape(
        length, prompts * state_size
    )
    table = jnp.transpose(initial, (0, 3, 1, 2)).reshape(prompts * state_size, heads * head_size)
    init_out = (
        jnp.dot(
            selected, table, precision=high_precision, preferred_element_type=jnp.float32
        ).reshape(length, heads, head_size)
        * from_begin[:, :, None]
    )
    mixed = intra_out + init_out + d_skip[None, :, None] * values
    gated = (
        mixed * jax.nn.silu(z_in.astype(jnp.float32).reshape(length, heads, head_size))
    ).reshape(length, heads * head_size)
    squares = jnp.broadcast_to(jnp.sum(gated * gated, axis=1, keepdims=True), (length, 128))
    scaled = (gated * norm_gain[None, :]).astype(jnp.bfloat16)
    hidden, query = project(
        scaled, squares, residual, attn_gain, q_up, out_weight, q_weight, q_down
    )
    ends = jnp.cumsum(lengths)
    finish = jnp.sum(jnp.where(onehot, ends[None, :], 0), axis=1)
    attended = attend_all(
        query,
        begin,
        finish,
        first,
        (cache_keys, cache_values, new_keys, new_values),
        behind,
        forward,
    )
    return (hidden, attended)


def solution(mesh):
    in_specs = (
        P(("seq", "tp"), None),
        P("seq", "tp"),
        P("seq", "tp"),
        P("seq", None),
        P("seq", "tp"),
        P(None, "tp"),
        P(),
        P(None, None, "tp"),
        P(),
        P(None, "tp", None, None),
        P("tp"),
        P("tp"),
        P("tp"),
        P("tp"),
        P("tp", None),
        P(),
        P(None, "tp"),
        P(),
        P(None, "tp"),
        P("seq", "tp"),
        P("seq", "tp"),
        P("seq", "tp"),
        P("seq", "tp"),
        P(),
    )
    out_specs = (P(("seq", "tp"), None), P("seq", "tp"))
    return jax.shard_map(
        per_device, mesh=mesh, in_specs=in_specs, out_specs=out_specs, check_vma=False
    )
```

```python
import functools

import jax
import jax.numpy as jnp
from jax import lax
from jax.experimental import pallas as pl
from jax.experimental.pallas import tpu as pltpu
from jax.sharding import PartitionSpec as P

HA = 224


EPS = 1e-05
NEG = -1e30


def shifted_2(value, axis, steps):
    count = lax.axis_size(axis)
    initial, last = (max(0, -steps), min(count, count - steps))
    pairs = [(source, source + steps) for source in range(initial, last)]
    return jax.tree.map(lambda a: lax.ppermute(a, axis, pairs), value)


def project_kernel(
    reach, relay, chain_ref, table_ref, taken_ref, selected_ref, growth_ref, intra_ref, conv_ref,
    skip_ref, z_ref, norm_ref, res_ref, gain_ref, up_ref, ow_hbm, qw_hbm, qd_hbm, *rest,
):
    if relay:
        y_back, y_fore, z_back, z_fore = rest[:4]
        hid_ref, query_ref, back_1, back_3, fore_1, fore_3 = rest[4:10]
        k_send, k_recv, k_local = rest[-3:]
        rest = rest[10:-3]
    else:
        hid_ref, query_ref = rest[:2]
        rest = rest[2:]
    project_body(
        reach, relay, (y_back, y_fore, z_back, z_fore, back_1, back_3, fore_1, fore_3, k_send, k_recv, k_local)
        if relay else None,
        chain_ref, table_ref, taken_ref, selected_ref, growth_ref, intra_ref, conv_ref,
        skip_ref, z_ref, norm_ref, res_ref, gain_ref, up_ref, ow_hbm, qw_hbm, qd_hbm,
        hid_ref, query_ref, *rest,
    )


def project_body(
    reach, relay, halo, chain_ref, table_ref, taken_ref, selected_ref, growth_ref, intra_ref, conv_ref,
    skip_ref, z_ref, norm_ref, res_ref, gain_ref, up_ref, ow_hbm, qw_hbm, qd_hbm,
    hid_ref, query_ref,
    st_recv, g_ref, sq_ref, s0, r0,
    ow, qw, qd, part, send1, recv1, send2, recv2, sq_recv, total, gathered, acc, low_acc,
    w_sem, s1, r1, s2, r2, s3, r3, s4, r4, s5, r5, s6, r6,
):
    me = lax.axis_index("tp")
    core, x = lax.rem(me, 2), me // 2
    mate = x * 2 + (1 - core)
    across = (1 - x) * 2 + core
    corner = (1 - x) * 2 + (1 - core)
    share = res_ref.shape[0]
    chunks, width = send2.shape[0], send2.shape[2]
    copies = [
        pltpu.make_async_copy(ow_hbm, ow, w_sem.at[0]),
        pltpu.make_async_copy(qw_hbm, qw, w_sem.at[1]),
        pltpu.make_async_copy(qd_hbm, qd, w_sem.at[2]),
    ]
    for copy in copies:
        copy.start()

    barrier = pltpu.get_barrier_semaphore()
    for other in (mate, across, corner):
        pl.semaphore_signal(
            barrier, inc=1, device_id={"tp": other}, device_id_type=pl.DeviceIdType.MESH
        )
    place = lax.axis_index("seq")
    count = lax.axis_size("seq")
    for distance in range(1, reach + 1):
        for other, near in (
            (place - distance, place >= distance),
            (place + distance, place + distance < count),
        ):

            @pl.when(near)
            def _():
                pl.semaphore_signal(
                    barrier, inc=1, device_id={"seq": other}, device_id_type=pl.DeviceIdType.MESH
                )

    peers = 3 + jnp.minimum(place, reach) + jnp.minimum(count - 1 - place, reach)
    pl.semaphore_wait(barrier, peers)

    def along(src, dst, send, recv, other):
        return pltpu.make_async_remote_copy(
            src_ref=src,
            dst_ref=dst,
            send_sem=send,
            recv_sem=recv,
            device_id={"seq": other},
            device_id_type=pl.DeviceIdType.MESH,
        )

    def state(distance, other):
        k = distance - 1
        return along(chain_ref, st_recv.at[k], s0.at[k], r0.at[k], other)

    for distance in range(1, reach + 1):

        @pl.when(place + distance < count)
        def _():
            state(distance, place + distance).start()

    if relay:
        y_back, y_fore, z_back, z_fore, back_1, back_3, fore_1, fore_3, k_send, k_recv, k_local = halo
        even = lax.rem(place, 2) == 0
        odd = lax.rem(place, 2) == 1
        kv = y_fore.shape[1] // 2

        def part_of(ref, j):
            return ref.at[:, pl.ds(j * kv, kv)]

        def back_in(j):
            return along(
                part_of(z_back, j), part_of(back_1, j), k_send.at[j], k_recv.at[j], place - 1
            )

        def fore_in(j):
            return along(
                part_of(z_fore, j), part_of(fore_1, j), k_send.at[j], k_recv.at[j], place + 1
            )

        def back_on(j):
            k = 4 + j
            return along(
                part_of(back_1, j), part_of(back_3, j), k_send.at[k], k_recv.at[k], place + 2
            )

        def fore_on(j):
            k = 8 + j
            return along(
                part_of(fore_1, j), part_of(fore_3, j), k_send.at[k], k_recv.at[k], place - 2
            )

        def back_own():
            return pltpu.make_async_copy(y_back, back_1, k_local.at[0])

        def fore_own():
            return pltpu.make_async_copy(y_fore, fore_1, k_local.at[0])

        @pl.when(odd)
        def _():
            back_own().start()
            for j in range(4):
                back_in(j).start()
            back_own().wait()
            for j in range(4):

                @pl.when(place + 2 < count)
                def _():
                    back_on(j).start()

        @pl.when(even)
        def _():
            fore_own().start()
            for j in range(2):
                fore_in(j).start()
            fore_own().wait()
            for j in range(2):

                @pl.when(place >= 2)
                def _():
                    fore_on(j).start()

        def forward_back(j):
            @pl.when(even)
            def _():
                back_in(j).wait_recv()

                @pl.when(place + 2 < count)
                def _():
                    back_on(j).start()

        def forward_fore(j):
            @pl.when(odd)
            def _():
                fore_in(j).wait_recv()

                @pl.when(place >= 2)
                def _():
                    fore_on(j).start()

        def finish_halo():
            @pl.when(odd)
            def _():
                for j in range(4):
                    back_in(j).wait_send()

            @pl.when(even)
            def _():
                for j in range(2):
                    fore_in(j).wait_send()

            for j in range(4):

                @pl.when(place + 2 < count)
                def _():
                    back_on(j).wait_send()

                @pl.when(place >= 2)
                def _():
                    back_on(j).wait_recv()

            for j in range(2):

                @pl.when(place >= 2)
                def _():
                    fore_on(j).wait_send()

                @pl.when(place + 2 < count)
                def _():
                    fore_on(j).wait_recv()

    carried = None
    size = chain_ref.shape[0] - 16
    for distance in range(reach, 0, -1):

        @pl.when(place >= distance)
        def _():
            state(distance, place + distance).wait_recv()

        @pl.when(place < distance)
        def _():
            st_recv[distance - 1] = jnp.zeros_like(st_recv[distance - 1])

        arrived = st_recv[distance - 1].astype(jnp.float32)
        if carried is None:
            carried = arrived[:size]
        else:
            carried = arrived[size : size + 1] * carried + arrived[:size]
    prompts = table_ref.shape[0] // size
    initial = jnp.where(
        taken_ref[:, :1] > 0, jnp.concatenate([carried] * prompts, axis=0), table_ref[...]
    )
    upper = initial.astype(jnp.bfloat16)
    lower = (initial - upper.astype(jnp.float32)).astype(jnp.bfloat16)
    picked = jnp.dot(selected_ref[...], upper, preferred_element_type=jnp.float32) + jnp.dot(
        selected_ref[...], lower, preferred_element_type=jnp.float32
    )
    mixed = (
        intra_ref[...]
        + picked * growth_ref[...]
        + skip_ref[...] * conv_ref[...].astype(jnp.float32)
    )
    gate = z_ref[...].astype(jnp.float32)
    gated = mixed * (gate * jax.nn.sigmoid(gate))
    g_ref[...] = (gated * norm_ref[...]).astype(jnp.bfloat16)
    sq_ref[...] = jnp.broadcast_to(jnp.sum(gated * gated, axis=1, keepdims=True), sq_ref.shape)

    def rows(owner):
        return pl.ds(pl.multiple_of(owner * share, share), share)

    def remote(src, dst, send, recv, other):
        return pltpu.make_async_remote_copy(
            src_ref=src,
            dst_ref=dst,
            send_sem=send,
            recv_sem=recv,
            device_id={"tp": other},
            device_id_type=pl.DeviceIdType.MESH,
        )

    sq_copies = [
        remote(sq_ref.at[rows(other)], sq_recv.at[k], s3.at[k], r3.at[k], other)
        for k, other in enumerate((mate, across, corner))
    ]
    for copy in sq_copies:
        copy.start()
    copies[0].wait()

    def first(i):
        return remote(send1.at[i], recv1.at[i], s1.at[i], r1.at[i], mate)

    def second(i):
        return remote(send2.at[i], recv2.at[i], s2.at[i], r2.at[i], across)

    def columns(i):
        return pl.ds(pl.multiple_of(i * width, width), width)

    @pl.loop(0, chunks)
    def _(i):
        cols = columns(i)
        part[:, cols] = jnp.dot(g_ref[...], ow[:, cols], preferred_element_type=jnp.float32)
        for half in range(2):
            send1[i, half] = part[rows(half * 2 + (1 - core)), cols].astype(jnp.bfloat16)
        first(i).start()

    @pl.loop(0, chunks)
    def _(i):
        first(i).wait()
        cols = columns(i)
        send2[i] = (
            part[rows(across), cols] + recv1[i, 1 - x].astype(jnp.float32)
        ).astype(jnp.bfloat16)
        second(i).start()

    if relay:
        forward_fore(0)
        forward_back(0)
    for copy in sq_copies:
        copy.wait()
    squares = sq_ref[rows(me)] + sq_recv[0] + sq_recv[1] + sq_recv[2]
    inner = g_ref.shape[1] * 4
    ratio = lax.rsqrt(squares[:, :1] / inner + EPS)

    @pl.loop(0, chunks)
    def _(i):
        second(i).wait()
        cols = columns(i)
        summed = (
            part[rows(me), cols]
            + recv1[i, x].astype(jnp.float32)
            + recv2[i].astype(jnp.float32)
        )
        hidden = (res_ref[:, cols].astype(jnp.float32) + ratio * summed).astype(jnp.bfloat16)
        hid_ref[:, cols] = hidden
        level = hidden.astype(jnp.float32)
        square = jnp.sum(level * level, axis=1, keepdims=True)
        total[...] = jnp.where(i == 0, square, total[...] + square)

    features = res_ref.shape[1]
    scale = lax.rsqrt(total[:, :1] / features + EPS)

    def over(i):
        place = (me, slice(None), columns(i))
        return remote(gathered.at[place], gathered.at[place], s4.at[i], r4.at[i], across)

    def beside(i):
        place = (me, slice(None), columns(i))
        return remote(gathered.at[place], gathered.at[place], s5.at[i], r5.at[i], mate)

    def onward(i):
        place = (across, slice(None), columns(i))
        return remote(gathered.at[place], gathered.at[place], s6.at[i], r6.at[i], mate)

    @pl.loop(0, chunks)
    def _(i):
        cols = columns(i)
        gathered[me, :, cols] = (
            hid_ref[:, cols].astype(jnp.float32) * scale * gain_ref[:, cols]
        ).astype(jnp.bfloat16)
        over(i).start()
        beside(i).start()

    if relay:
        forward_back(1)
        forward_fore(1)

    @pl.loop(0, chunks)
    def _(i):
        over(i).wait_recv()
        onward(i).start()

    if relay:
        forward_back(2)
        forward_back(3)
    copies[1].wait()
    copies[2].wait()

    @pl.loop(0, chunks)
    def _(i):
        over(i).wait_send()
        beside(i).wait()
        onward(i).wait()
        cols = columns(i)
        block = gathered[:, :, cols].reshape(4 * share, width)
        product = jnp.dot(block, qw[cols, :], preferred_element_type=jnp.float32)
        adapted = jnp.dot(block, qd[cols, :], preferred_element_type=jnp.float32)
        acc[...] = jnp.where(i == 0, product, acc[...] + product)
        low_acc[...] = jnp.where(i == 0, adapted, low_acc[...] + adapted)

    for distance in range(1, reach + 1):

        @pl.when(place + distance < count)
        def _():
            state(distance, place + distance).wait_send()

    if relay:
        finish_halo()
    low = low_acc[...].astype(jnp.bfloat16)
    query_ref[...] = (
        acc[...] + jnp.dot(low, up_ref[...], preferred_element_type=jnp.float32)
    ).astype(jnp.bfloat16)


def project(
    reach, parts, residual, attn_gain, q_up, out_weight, q_weight, q_down, halo
):
    chain, intra = parts[0], parts[5]
    relay = halo is not None
    share, features = residual.shape
    length, inner = intra.shape
    columns, rank = q_weight.shape[1], q_down.shape[1]
    width = 512
    chunks = features // width
    bf, f32 = jnp.bfloat16, jnp.float32
    vmem = pl.BlockSpec(memory_space=pltpu.VMEM)
    hbm = pl.BlockSpec(memory_space=pl.ANY)
    dma = pltpu.SemaphoreType.DMA
    extra = tuple(halo) if relay else ()
    halo_out = ()
    if relay:
        wide = jax.ShapeDtypeStruct(halo[0].shape, bf)
        narrow = jax.ShapeDtypeStruct(halo[1].shape, bf)
        halo_out = (wide, wide, narrow, narrow)
    return pl.pallas_call(
        functools.partial(project_kernel, reach, relay),
        out_shape=(
            jax.ShapeDtypeStruct((share, features), bf),
            jax.ShapeDtypeStruct((length, columns), bf),
        )
        + halo_out,
        in_specs=[vmem] * (len(parts) + 3) + [hbm] * (3 + len(extra)),
        out_specs=(vmem, vmem) + (hbm,) * len(halo_out),
        scratch_shapes=[
            pltpu.VMEM((reach,) + chain.shape, bf),
            pltpu.VMEM((length, inner), bf),
            pltpu.VMEM((length, 128), f32),
            dma((reach,)),
            dma((reach,)),
            pltpu.VMEM(out_weight.shape, bf),
            pltpu.VMEM(q_weight.shape, bf),
            pltpu.VMEM(q_down.shape, bf),
            pltpu.VMEM((length, features), f32),
            pltpu.VMEM((chunks, 2, share, width), bf),
            pltpu.VMEM((chunks, 2, share, width), bf),
            pltpu.VMEM((chunks, share, width), bf),
            pltpu.VMEM((chunks, share, width), bf),
            pltpu.VMEM((3, share, 128), f32),
            pltpu.VMEM((share, 128), f32),
            pltpu.VMEM((4, share, features), bf),
            pltpu.VMEM((length, columns), f32),
            pltpu.VMEM((length, rank), f32),
            dma((3,)),
        ]
        + [dma((chunks,))] * 4
        + [dma((3,))] * 2
        + [dma((chunks,))] * 6
        + ([dma((10,)), dma((10,)), dma((1,))] if relay else []),
        compiler_params=pltpu.CompilerParams(
            collective_id=0, has_side_effects=True, vmem_limit_bytes=48 * 2**20
        ),
        cost_estimate=pl.CostEstimate(
            flops=4 * length * inner * features, bytes_accessed=400 * 2**20, transcendentals=0
        ),
        name="project",
    )(
        *parts, residual, attn_gain.reshape(1, features), q_up, out_weight, q_weight, q_down, *extra
    )


def attend_kernel(offsets, near_ref, query_ref, begin_ref, end_ref, *refs):
    pieces = refs[: -4]
    out_ref, acc, top_ref, sum_ref = refs[-4:]
    length, width = query_ref.shape
    heads = width // HA
    scale = 1.0 / HA**0.5
    first = near_ref[0]
    low, high = near_ref[1], near_ref[2]
    lanes = lax.broadcasted_iota(jnp.int32, (length, length), 1)
    own = lax.broadcasted_iota(jnp.int32, (length, length), 0)
    windows = []
    for head in range(heads):
        left = head * HA // 128 * 128
        right = -(-(head + 1) * HA // 128) * 128
        windows.append((left, right))
    top_ref[...] = jnp.full_like(top_ref, NEG)
    sum_ref[...] = jnp.zeros_like(sum_ref)
    acc[...] = jnp.zeros_like(acc)

    def member(head):
        left, right = windows[head]
        column = left + lax.broadcasted_iota(jnp.int32, (length, right - left), 1)
        return (column >= head * HA) & (column < (head + 1) * HA)

    def visit(keys, values, offset, causal):
        start = first + offset * length
        index = start + lanes
        mask = (index >= begin_ref[:, :1]) & (index < end_ref[:, :1])
        if causal:
            mask = mask & (index <= first + own)
        for head in range(heads):
            left, right = windows[head]
            query = jnp.where(member(head), query_ref[:, left:right], jnp.bfloat16(0))
            scores = (
                lax.dot_general(
                    query,
                    keys[0][:, keys[1] + left : keys[1] + right],
                    (((1,), (1,)), ((), ())),
                    preferred_element_type=jnp.float32,
                )
                * scale
            )
            scores = jnp.where(mask, scores, NEG)
            old = top_ref[head][:, :1]
            top = jnp.maximum(old, jnp.max(scores, axis=1, keepdims=True))
            weights = jnp.exp(scores - top)
            shrink = jnp.exp(old - top)
            shape = (length, 128)
            top_ref[head] = jnp.broadcast_to(top, shape)
            sum_ref[head] = sum_ref[head] * shrink + jnp.sum(weights, axis=1, keepdims=True)
            acc[head, :, : right - left] = acc[head, :, : right - left] * shrink + jnp.dot(
                weights.astype(jnp.bfloat16),
                values[0][:, values[1] + left : values[1] + right],
                preferred_element_type=jnp.float32,
            )

    def entry(piece, part):
        if piece < 0:
            return (pieces[part], 0)
        return (pieces[4 + piece], part * width)

    for place, (piece, offset, causal) in enumerate(offsets):
        part = 2 if causal else 0
        keys, values = entry(piece, part), entry(piece, part + 1)
        start = first + offset * length
        if offset == 0:
            visit(keys, values, offset, causal)
        else:
            pl.when((start < high) & (start + length > low))(
                functools.partial(visit, keys, values, offset, causal)
            )
    for head in range(heads):
        left, right = windows[head]
        result = acc[head, :, : right - left] / sum_ref[head][:, :1]
        result = result.astype(jnp.bfloat16)
        if head == 0:
            out_ref[:, left:right] = result
        else:
            shared = windows[head - 1][1]
            kept = jnp.where(
                member(head)[:, : shared - left], result[:, : shared - left], out_ref[:, left:shared]
            )
            out_ref[:, left:shared] = kept
            out_ref[:, shared:right] = result[:, shared - left :]


def attend_all(query, begin, end, first, own, behind, forward):
    length, width = query.shape
    heads = width // HA
    offsets = [(-1, 0, False), (-1, 0, True)]
    for place in range(len(behind)):
        offsets += [(place, -place - 1, False), (place, -place - 1, True)]
    for place in range(len(forward)):
        offsets.append((len(behind) + place, place + 1, False))
    low, high = begin[0], end[length - 1]
    near = jnp.stack([first, low, high]).astype(jnp.int32)
    spread = lambda a: jnp.broadcast_to(a[:, None], (length, 128)).astype(jnp.int32)
    vmem = pl.BlockSpec(memory_space=pltpu.VMEM)
    return pl.pallas_call(
        functools.partial(attend_kernel, tuple(offsets)),
        out_shape=jax.ShapeDtypeStruct((length, width), jnp.bfloat16),
        in_specs=[pl.BlockSpec(memory_space=pltpu.SMEM)]
        + [vmem] * (3 + 4 + len(behind) + len(forward)),
        out_specs=vmem,
        scratch_shapes=[
            pltpu.VMEM((heads, length, 384), jnp.float32),
            pltpu.VMEM((heads, length, 128), jnp.float32),
            pltpu.VMEM((heads, length, 128), jnp.float32),
        ],
        compiler_params=pltpu.CompilerParams(vmem_limit_bytes=48 * 2**20),
        name="attend",
    )(near, query, spread(begin), spread(end), *own, *behind, *forward)


def locate(lengths, index):
    ends = jnp.cumsum(lengths)
    starts = ends - lengths
    count = lengths.shape[0]
    segment = jnp.sum((index[:, None] >= ends[None, :]).astype(jnp.int32), axis=1)
    segment = jnp.minimum(segment, count - 1)
    onehot = segment[:, None] == jnp.arange(count, dtype=jnp.int32)[None, :]
    begin = jnp.sum(jnp.where(onehot, starts[None, :], 0), axis=1)
    valid = (index >= 0) & (index < ends[count - 1])
    return (segment, begin, valid, onehot)


def convolve(inputs, border, cache, weight, position, onehot):
    taps = weight.shape[0]
    length = inputs.shape[0]
    extended = jnp.concatenate([border, inputs], axis=0)
    picks = onehot.astype(jnp.bfloat16)
    cached_rows = [
        jnp.dot(picks, cache[:, slot, :], preferred_element_type=jnp.float32)
        for slot in range(taps - 1)
    ]
    result = weight[0][None, :] * inputs.astype(jnp.float32)
    for lag in range(1, taps):
        shifted = extended[taps - 1 - lag : taps - 1 - lag + length].astype(jnp.float32)
        slot_index = taps - 1 + position - lag
        fallback = jnp.zeros_like(shifted)
        for slot in range(taps - 1):
            fallback = jnp.where((slot_index == slot)[:, None], cached_rows[slot], fallback)
        shifted = jnp.where((position >= lag)[:, None], shifted, fallback)
        result = result + weight[lag][None, :] * shifted
    return jax.nn.silu(result).astype(jnp.bfloat16)


def per_device(
    residual,
    x_in,
    z_in,
    bc_in,
    dt_in,
    conv_x_weight,
    conv_bc_weight,
    conv_x_cache,
    conv_bc_cache,
    ssm_cache,
    dt_bias,
    a_log,
    d_skip,
    norm_gain,
    out_weight,
    attn_gain,
    q_weight,
    q_down,
    q_up,
    cache_keys,
    cache_values,
    new_keys,
    new_values,
    lengths,
):
    high_precision = lax.Precision.HIGH
    length = x_in.shape[0]
    taps = conv_x_weight.shape[0]
    seq_index = lax.axis_index("seq")
    seq_count = lax.axis_size("seq")
    reach = seq_count // 4 + 1
    first = seq_index * length
    packed = jnp.concatenate([cache_keys, cache_values, new_keys, new_values], axis=1)
    packed_cache = packed[:, : 2 * cache_keys.shape[1]]
    relay = reach == 3 and seq_count % 2 == 0
    if relay:
        pairs = range(0, seq_count, 2)
        halo = (
            lax.ppermute(packed, "seq", [(s, s + 1) for s in pairs]),
            lax.ppermute(packed_cache, "seq", [(s + 1, s) for s in pairs]),
            shifted_2(packed, "seq", 2),
            shifted_2(packed_cache, "seq", -2),
        )
    else:
        halo = None
        behind = [shifted_2(packed, "seq", distance) for distance in range(1, reach + 1)]
        forward = [shifted_2(packed_cache, "seq", -distance) for distance in range(1, reach + 1)]
    local_index = first + jnp.arange(length, dtype=jnp.int32)
    segment, begin, valid, onehot = locate(lengths, local_index)
    position = local_index - begin
    border = shifted_2(
        jnp.concatenate([x_in[length - taps + 1 :], bc_in[length - taps + 1 :]], axis=1), "seq", 1
    )
    x_border, bc_border = border[:, : x_in.shape[1]], border[:, x_in.shape[1] :]
    x_conv = convolve(x_in, x_border, conv_x_cache, conv_x_weight, position, onehot)
    bc_conv = convolve(bc_in, bc_border, conv_bc_cache, conv_bc_weight, position, onehot)
    heads = dt_bias.shape[0]
    state_size = bc_in.shape[1] // 2
    head_size = x_in.shape[1] // heads
    prompts = lengths.shape[0]
    values_bf = x_conv.reshape(length, heads, head_size)
    values = x_conv.astype(jnp.float32).reshape(length, heads, head_size)
    inputs_b = bc_conv[:, :state_size]
    inputs_c = bc_conv[:, state_size:]
    step = jax.nn.softplus(dt_in + dt_bias[None, :])
    log_decay = -step * jnp.exp(a_log)[None, :]
    cumulative = jnp.cumsum(log_decay, axis=0)
    local_begin = jnp.maximum(begin - first, 0)
    before = jnp.take(cumulative - log_decay, local_begin, axis=0)
    from_begin = jnp.exp(cumulative - before)
    block = min(length, 512)
    pair_scores = jnp.dot(inputs_c, inputs_b.T, preferred_element_type=jnp.float32)
    cumulative_t = cumulative.T
    step_t = step.T
    order = jnp.arange(length, dtype=jnp.int32)

    def intra(block_start):
        query_rows = block_start + jnp.arange(block, dtype=jnp.int32)
        same = (segment[:, None] == segment[None, :]) & (query_rows[:, None] >= order[None, :])
        gap = cumulative_t[:, :, None] - cumulative_t[:, None, :]
        factor = jnp.where(same[None], jnp.exp(jnp.where(same[None], gap, 0.0)), 0.0)
        weights = factor * step_t[:, None, :] * pair_scores[None, :, :]
        return jnp.einsum(
            "hqs,shd->qhd",
            weights,
            values_bf,
            precision=high_precision,
            preferred_element_type=jnp.float32,
        )

    intra_out = lax.map(intra, jnp.arange(length // block, dtype=jnp.int32) * block).reshape(
        length, heads, head_size
    )
    last_segment = segment[length - 1]
    in_last = segment == last_segment
    tail_weight = (
        jnp.where(in_last[:, None], jnp.exp(cumulative[length - 1][None, :] - cumulative), 0.0)
        * step
    )
    inner = heads * head_size
    spread = jnp.repeat(jnp.eye(heads, dtype=jnp.float32), head_size, axis=1)

    def widen(per_head):
        return jnp.dot(per_head, spread, precision=lax.Precision.HIGHEST)

    local_state = lax.dot_general(
        inputs_b.astype(jnp.float32),
        widen(tail_weight) * x_conv.astype(jnp.float32),
        (((0,), (0,)), ((), ())),
        precision=high_precision,
        preferred_element_type=jnp.float32,
    )
    whole_decay = jnp.exp(cumulative[length - 1] - before[length - 1])
    starts_here = begin[length - 1] >= first
    table = jnp.transpose(ssm_cache, (0, 3, 1, 2)).reshape(prompts, state_size, inner)
    cached_last = lax.dynamic_index_in_dim(table, last_segment, 0, keepdims=False)
    wide_decay = jnp.repeat(whole_decay, head_size)[None, :]
    chain_state = local_state + jnp.where(starts_here, wide_decay * cached_last, 0.0)
    chain_decay = jnp.where(starts_here, jnp.zeros_like(wide_decay), wide_decay)
    chain = jnp.concatenate(
        [chain_state, jnp.broadcast_to(chain_decay, (16, inner))], axis=0
    ).astype(jnp.bfloat16)
    continuing = position[0] > 0
    replace = (jnp.arange(prompts, dtype=jnp.int32) == segment[0]) & continuing
    taken = jnp.broadcast_to(
        jnp.repeat(replace.astype(jnp.float32), state_size)[:, None], (prompts * state_size, 128)
    )
    selected = (onehot[:, :, None].astype(jnp.bfloat16) * inputs_c[:, None, :]).reshape(
        length, prompts * state_size
    )
    parts = (
        chain,
        table.reshape(prompts * state_size, inner),
        taken,
        selected,
        widen(from_begin),
        intra_out.reshape(length, inner),
        x_conv,
        jnp.repeat(d_skip, head_size)[None, :],
        z_in,
        norm_gain[None, :],
    )
    hidden, query, *arrived = project(
        reach, parts, residual, attn_gain, q_up, out_weight, q_weight, q_down, halo
    )
    if relay:
        behind = (arrived[0], halo[2], arrived[1])
        forward = (arrived[2], halo[3], arrived[3])
    ends = jnp.cumsum(lengths)
    finish = jnp.sum(jnp.where(onehot, ends[None, :], 0), axis=1)
    attended = attend_all(
        query,
        begin,
        finish,
        first,
        (cache_keys, cache_values, new_keys, new_values),
        behind,
        forward,
    )
    return (hidden, attended)


def solution(mesh):
    in_specs = (
        P(("seq", "tp"), None),
        P("seq", "tp"),
        P("seq", "tp"),
        P("seq", None),
        P("seq", "tp"),
        P(None, "tp"),
        P(),
        P(None, None, "tp"),
        P(),
        P(None, "tp", None, None),
        P("tp"),
        P("tp"),
        P("tp"),
        P("tp"),
        P("tp", None),
        P(),
        P(None, "tp"),
        P(),
        P(None, "tp"),
        P("seq", "tp"),
        P("seq", "tp"),
        P("seq", "tp"),
        P("seq", "tp"),
        P(),
    )
    out_specs = (P(("seq", "tp"), None), P("seq", "tp"))
    return jax.shard_map(
        per_device, mesh=mesh, in_specs=in_specs, out_specs=out_specs, check_vma=False
    )
```

```python
import functools

import jax
import jax.numpy as jnp
from jax import lax
from jax.experimental import pallas as pl
from jax.experimental.pallas import tpu as pltpu
from jax.sharding import PartitionSpec as P

HA = 224


EPS = 1e-05
NEG = -1e30


def shifted_2(value, axis, steps):
    count = lax.axis_size(axis)
    initial, last = (max(0, -steps), min(count, count - steps))
    pairs = [(source, source + steps) for source in range(initial, last)]
    return jax.tree.map(lambda a: lax.ppermute(a, axis, pairs), value)


def project_kernel(
    reach, relay, chain_ref, table_ref, taken_ref, selected_ref, growth_ref, intra_ref, conv_ref,
    skip_ref, z_ref, norm_ref, res_ref, gain_ref, up_ref, ow_hbm, qw_hbm, qd_hbm, *rest,
):
    if relay:
        y_back, y_fore, z_back, z_fore = rest[:4]
        hid_ref, query_ref, back_1, back_3, fore_1, fore_3 = rest[4:10]
        k_send, k_recv = rest[-2:]
        rest = rest[10:-2]
    else:
        hid_ref, query_ref = rest[:2]
        rest = rest[2:]
    project_body(
        reach, relay, (y_back, y_fore, z_back, z_fore, back_1, back_3, fore_1, fore_3, k_send, k_recv)
        if relay else None,
        chain_ref, table_ref, taken_ref, selected_ref, growth_ref, intra_ref, conv_ref,
        skip_ref, z_ref, norm_ref, res_ref, gain_ref, up_ref, ow_hbm, qw_hbm, qd_hbm,
        hid_ref, query_ref, *rest,
    )


def project_body(
    reach, relay, halo, chain_ref, table_ref, taken_ref, selected_ref, growth_ref, intra_ref, conv_ref,
    skip_ref, z_ref, norm_ref, res_ref, gain_ref, up_ref, ow_hbm, qw_hbm, qd_hbm,
    hid_ref, query_ref,
    st_recv, g_ref, sq_ref, s0, r0,
    ow, qw, qd, part, send1, recv1, send2, recv2, sq_recv, total, gathered, acc, low_acc,
    w_sem, s1, r1, s2, r2, s3, r3, s4, r4, s5, r5, s6, r6,
):
    me = lax.axis_index("tp")
    core, x = lax.rem(me, 2), me // 2
    mate = x * 2 + (1 - core)
    across = (1 - x) * 2 + core
    corner = (1 - x) * 2 + (1 - core)
    share = res_ref.shape[0]
    chunks, width = send2.shape[0], send2.shape[2]
    copies = [
        pltpu.make_async_copy(ow_hbm, ow, w_sem.at[0]),
        pltpu.make_async_copy(qw_hbm, qw, w_sem.at[1]),
        pltpu.make_async_copy(qd_hbm, qd, w_sem.at[2]),
    ]
    for copy in copies:
        copy.start()

    barrier = pltpu.get_barrier_semaphore()
    for other in (mate, across, corner):
        pl.semaphore_signal(
            barrier, inc=1, device_id={"tp": other}, device_id_type=pl.DeviceIdType.MESH
        )
    place = lax.axis_index("seq")
    count = lax.axis_size("seq")
    for distance in range(1, reach + 1):
        for other, near in (
            (place - distance, place >= distance),
            (place + distance, place + distance < count),
        ):

            @pl.when(near)
            def _():
                pl.semaphore_signal(
                    barrier, inc=1, device_id={"seq": other}, device_id_type=pl.DeviceIdType.MESH
                )

    peers = 3 + jnp.minimum(place, reach) + jnp.minimum(count - 1 - place, reach)
    pl.semaphore_wait(barrier, peers)

    def along(src, dst, send, recv, other):
        return pltpu.make_async_remote_copy(
            src_ref=src,
            dst_ref=dst,
            send_sem=send,
            recv_sem=recv,
            device_id={"seq": other},
            device_id_type=pl.DeviceIdType.MESH,
        )

    def state(distance, other):
        k = distance - 1
        return along(chain_ref, st_recv.at[k], s0.at[k], r0.at[k], other)

    for distance in range(1, reach + 1):

        @pl.when(place + distance < count)
        def _():
            state(distance, place + distance).start()

    if relay:
        y_back, y_fore, z_back, z_fore, back_1, back_3, fore_1, fore_3, k_send, k_recv = halo
        even = lax.rem(place, 2) == 0
        odd = lax.rem(place, 2) == 1
        kv = y_fore.shape[1] // 2

        def part_of(ref, j):
            return ref.at[:, pl.ds(j * kv, kv)]

        def back_in(j):
            return along(
                part_of(z_back, j), part_of(back_1, j), k_send.at[j], k_recv.at[j], place - 1
            )

        def fore_in(j):
            return along(
                part_of(z_fore, j), part_of(fore_1, j), k_send.at[j], k_recv.at[j], place + 1
            )

        def back_on(j, src=None):
            k = 4 + j
            return along(
                part_of(back_1 if src is None else src, j), part_of(back_3, j), k_send.at[k], k_recv.at[k], place + 2
            )

        def fore_on(j, src=None):
            k = 8 + j
            return along(
                part_of(fore_1 if src is None else src, j), part_of(fore_3, j), k_send.at[k], k_recv.at[k], place - 2
            )

        @pl.when(odd)
        def _():
            for j in range(4):
                back_in(j).start()

                @pl.when(place + 2 < count)
                def _():
                    back_on(j, y_back).start()

        @pl.when(even)
        def _():
            for j in range(2):
                fore_in(j).start()

                @pl.when(place >= 2)
                def _():
                    fore_on(j, y_fore).start()

        def forward_back(j):
            @pl.when(even)
            def _():
                back_in(j).wait_recv()

                @pl.when(place + 2 < count)
                def _():
                    back_on(j).start()

        def forward_fore(j):
            @pl.when(odd)
            def _():
                fore_in(j).wait_recv()

                @pl.when(place >= 2)
                def _():
                    fore_on(j).start()

        def finish_halo():
            @pl.when(odd)
            def _():
                for j in range(4):
                    back_in(j).wait_send()

            @pl.when(even)
            def _():
                for j in range(2):
                    fore_in(j).wait_send()

            for j in range(4):

                @pl.when(place + 2 < count)
                def _():
                    back_on(j).wait_send()

                @pl.when(place >= 2)
                def _():
                    back_on(j).wait_recv()

            for j in range(2):

                @pl.when(place >= 2)
                def _():
                    fore_on(j).wait_send()

                @pl.when(place + 2 < count)
                def _():
                    fore_on(j).wait_recv()

    carried = None
    size = chain_ref.shape[0] - 16
    for distance in range(reach, 0, -1):

        @pl.when(place >= distance)
        def _():
            state(distance, place + distance).wait_recv()

        @pl.when(place < distance)
        def _():
            st_recv[distance - 1] = jnp.zeros_like(st_recv[distance - 1])

        arrived = st_recv[distance - 1].astype(jnp.float32)
        if carried is None:
            carried = arrived[:size]
        else:
            carried = arrived[size : size + 1] * carried + arrived[:size]
    prompts = table_ref.shape[0] // size
    initial = jnp.where(
        taken_ref[:, :1] > 0, jnp.concatenate([carried] * prompts, axis=0), table_ref[...]
    )
    upper = initial.astype(jnp.bfloat16)
    lower = (initial - upper.astype(jnp.float32)).astype(jnp.bfloat16)
    picked = jnp.dot(selected_ref[...], upper, preferred_element_type=jnp.float32) + jnp.dot(
        selected_ref[...], lower, preferred_element_type=jnp.float32
    )
    mixed = (
        intra_ref[...]
        + picked * growth_ref[...]
        + skip_ref[...] * conv_ref[...].astype(jnp.float32)
    )
    gate = z_ref[...].astype(jnp.float32)
    gated = mixed * (gate * jax.nn.sigmoid(gate))
    g_ref[...] = (gated * norm_ref[...]).astype(jnp.bfloat16)
    sq_ref[...] = jnp.broadcast_to(jnp.sum(gated * gated, axis=1, keepdims=True), sq_ref.shape)

    if relay:
        forward_fore(0)
        forward_back(0)

    def rows(owner):
        return pl.ds(pl.multiple_of(owner * share, share), share)

    def remote(src, dst, send, recv, other):
        return pltpu.make_async_remote_copy(
            src_ref=src,
            dst_ref=dst,
            send_sem=send,
            recv_sem=recv,
            device_id={"tp": other},
            device_id_type=pl.DeviceIdType.MESH,
        )

    sq_copies = [
        remote(sq_ref.at[rows(other)], sq_recv.at[k], s3.at[k], r3.at[k], other)
        for k, other in enumerate((mate, across, corner))
    ]
    for copy in sq_copies:
        copy.start()
    copies[0].wait()

    def first(i):
        return remote(send1.at[i], recv1.at[i], s1.at[i], r1.at[i], mate)

    def second(i):
        return remote(send2.at[i], recv2.at[i], s2.at[i], r2.at[i], across)

    def columns(i):
        return pl.ds(pl.multiple_of(i * width, width), width)

    @pl.loop(0, chunks)
    def _(i):
        cols = columns(i)
        part[:, cols] = jnp.dot(g_ref[...], ow[:, cols], preferred_element_type=jnp.float32)
        for half in range(2):
            send1[i, half] = part[rows(half * 2 + (1 - core)), cols].astype(jnp.bfloat16)
        first(i).start()

    @pl.loop(0, chunks)
    def _(i):
        first(i).wait()
        cols = columns(i)
        send2[i] = (
            part[rows(across), cols] + recv1[i, 1 - x].astype(jnp.float32)
        ).astype(jnp.bfloat16)
        second(i).start()

    if relay:
        forward_fore(1)

    if relay:
        forward_back(1)
    for copy in sq_copies:
        copy.wait()
    squares = sq_ref[rows(me)] + sq_recv[0] + sq_recv[1] + sq_recv[2]
    inner = g_ref.shape[1] * 4
    ratio = lax.rsqrt(squares[:, :1] / inner + EPS)

    @pl.loop(0, chunks)
    def _(i):
        second(i).wait()
        cols = columns(i)
        summed = (
            part[rows(me), cols]
            + recv1[i, x].astype(jnp.float32)
            + recv2[i].astype(jnp.float32)
        )
        hidden = (res_ref[:, cols].astype(jnp.float32) + ratio * summed).astype(jnp.bfloat16)
        hid_ref[:, cols] = hidden
        level = hidden.astype(jnp.float32)
        square = jnp.sum(level * level, axis=1, keepdims=True)
        total[...] = jnp.where(i == 0, square, total[...] + square)

    features = res_ref.shape[1]
    scale = lax.rsqrt(total[:, :1] / features + EPS)

    def over(i):
        place = (me, slice(None), columns(i))
        return remote(gathered.at[place], gathered.at[place], s4.at[i], r4.at[i], across)

    def beside(i):
        place = (me, slice(None), columns(i))
        return remote(gathered.at[place], gathered.at[place], s5.at[i], r5.at[i], mate)

    def onward(i):
        place = (across, slice(None), columns(i))
        return remote(gathered.at[place], gathered.at[place], s6.at[i], r6.at[i], mate)

    @pl.loop(0, chunks)
    def _(i):
        cols = columns(i)
        gathered[me, :, cols] = (
            hid_ref[:, cols].astype(jnp.float32) * scale * gain_ref[:, cols]
        ).astype(jnp.bfloat16)
        over(i).start()
        beside(i).start()

    if relay:
        forward_back(2)

    @pl.loop(0, chunks)
    def _(i):
        over(i).wait_recv()
        onward(i).start()

    if relay:
        forward_back(3)
    copies[1].wait()
    copies[2].wait()

    @pl.loop(0, chunks)
    def _(i):
        over(i).wait_send()
        beside(i).wait()
        onward(i).wait()
        cols = columns(i)
        block = gathered[:, :, cols].reshape(4 * share, width)
        product = jnp.dot(block, qw[cols, :], preferred_element_type=jnp.float32)
        adapted = jnp.dot(block, qd[cols, :], preferred_element_type=jnp.float32)
        acc[...] = jnp.where(i == 0, product, acc[...] + product)
        low_acc[...] = jnp.where(i == 0, adapted, low_acc[...] + adapted)

    for distance in range(1, reach + 1):

        @pl.when(place + distance < count)
        def _():
            state(distance, place + distance).wait_send()

    if relay:
        finish_halo()
    low = low_acc[...].astype(jnp.bfloat16)
    query_ref[...] = (
        acc[...] + jnp.dot(low, up_ref[...], preferred_element_type=jnp.float32)
    ).astype(jnp.bfloat16)


def project(
    reach, parts, residual, attn_gain, q_up, out_weight, q_weight, q_down, halo
):
    chain, intra = parts[0], parts[5]
    relay = halo is not None
    share, features = residual.shape
    length, inner = intra.shape
    columns, rank = q_weight.shape[1], q_down.shape[1]
    width = 512
    chunks = features // width
    bf, f32 = jnp.bfloat16, jnp.float32
    vmem = pl.BlockSpec(memory_space=pltpu.VMEM)
    hbm = pl.BlockSpec(memory_space=pl.ANY)
    dma = pltpu.SemaphoreType.DMA
    extra = tuple(halo) if relay else ()
    halo_out = ()
    if relay:
        wide = jax.ShapeDtypeStruct(halo[0].shape, bf)
        narrow = jax.ShapeDtypeStruct(halo[1].shape, bf)
        halo_out = (wide, wide, narrow, narrow)
    return pl.pallas_call(
        functools.partial(project_kernel, reach, relay),
        out_shape=(
            jax.ShapeDtypeStruct((share, features), bf),
            jax.ShapeDtypeStruct((length, columns), bf),
        )
        + halo_out,
        in_specs=[vmem] * (len(parts) + 3) + [hbm] * (3 + len(extra)),
        out_specs=(vmem, vmem) + (hbm,) * len(halo_out),
        scratch_shapes=[
            pltpu.VMEM((reach,) + chain.shape, bf),
            pltpu.VMEM((length, inner), bf),
            pltpu.VMEM((length, 128), f32),
            dma((reach,)),
            dma((reach,)),
            pltpu.VMEM(out_weight.shape, bf),
            pltpu.VMEM(q_weight.shape, bf),
            pltpu.VMEM(q_down.shape, bf),
            pltpu.VMEM((length, features), f32),
            pltpu.VMEM((chunks, 2, share, width), bf),
            pltpu.VMEM((chunks, 2, share, width), bf),
            pltpu.VMEM((chunks, share, width), bf),
            pltpu.VMEM((chunks, share, width), bf),
            pltpu.VMEM((3, share, 128), f32),
            pltpu.VMEM((share, 128), f32),
            pltpu.VMEM((4, share, features), bf),
            pltpu.VMEM((length, columns), f32),
            pltpu.VMEM((length, rank), f32),
            dma((3,)),
        ]
        + [dma((chunks,))] * 4
        + [dma((3,))] * 2
        + [dma((chunks,))] * 6
        + ([dma((10,)), dma((10,))] if relay else []),
        compiler_params=pltpu.CompilerParams(
            collective_id=0, has_side_effects=True, vmem_limit_bytes=48 * 2**20
        ),
        cost_estimate=pl.CostEstimate(
            flops=4 * length * inner * features, bytes_accessed=400 * 2**20, transcendentals=0
        ),
        name="project",
    )(
        *parts, residual, attn_gain.reshape(1, features), q_up, out_weight, q_weight, q_down, *extra
    )


def attend_kernel(offsets, near_ref, query_ref, begin_ref, end_ref, *refs):
    pieces = refs[:-5]
    out_ref, acc, top_ref, sum_ref, masked = refs[-5:]
    length, width = query_ref.shape
    heads = width // HA
    scale = 1.0 / HA**0.5
    first = near_ref[0]
    low, high = near_ref[1], near_ref[2]
    lanes = lax.broadcasted_iota(jnp.int32, (length, length), 1)
    own = lax.broadcasted_iota(jnp.int32, (length, length), 0)
    windows = []
    for head in range(heads):
        left = head * HA // 128 * 128
        right = -(-(head + 1) * HA // 128) * 128
        windows.append((left, right))
    top_ref[...] = jnp.full_like(top_ref, NEG)
    sum_ref[...] = jnp.zeros_like(sum_ref)
    acc[...] = jnp.zeros_like(acc)

    def member(head):
        left, right = windows[head]
        column = left + lax.broadcasted_iota(jnp.int32, (length, right - left), 1)
        return (column >= head * HA) & (column < (head + 1) * HA)

    for head in range(heads):
        left, right = windows[head]
        masked[head, :, : right - left] = jnp.where(
            member(head), query_ref[:, left:right], jnp.bfloat16(0)
        )

    def visit(keys, values, offset, causal):
        start = first + offset * length
        index = start + lanes
        mask = (index >= begin_ref[:, :1]) & (index < end_ref[:, :1])
        if causal:
            mask = mask & (index <= first + own)
        for head in range(heads):
            left, right = windows[head]
            query = masked[head, :, : right - left]
            scores = (
                lax.dot_general(
                    query,
                    keys[0][:, keys[1] + left : keys[1] + right],
                    (((1,), (1,)), ((), ())),
                    preferred_element_type=jnp.float32,
                )
                * scale
            )
            scores = jnp.where(mask, scores, NEG)
            old = top_ref[head][:, :1]
            top = jnp.maximum(old, jnp.max(scores, axis=1, keepdims=True))
            weights = jnp.exp(scores - top)
            shrink = jnp.exp(old - top)
            shape = (length, 128)
            top_ref[head] = jnp.broadcast_to(top, shape)
            sum_ref[head] = sum_ref[head] * shrink + jnp.sum(weights, axis=1, keepdims=True)
            acc[head, :, : right - left] = acc[head, :, : right - left] * shrink + jnp.dot(
                weights.astype(jnp.bfloat16),
                values[0][:, values[1] + left : values[1] + right],
                preferred_element_type=jnp.float32,
            )

    def entry(piece, part):
        if piece < 0:
            return (pieces[part], 0)
        return (pieces[4 + piece], part * width)

    for piece, offset, causal, parity in offsets:
        part = 2 if causal else 0
        keys, values = entry(piece, part), entry(piece, part + 1)
        start = first + offset * length
        if offset == 0:
            visit(keys, values, offset, causal)
        else:
            wanted = (start < high) & (start + length > low)
            if parity is not None:
                wanted = wanted & (near_ref[3] == parity)
            pl.when(wanted)(
                functools.partial(visit, keys, values, offset, causal)
            )
    for head in range(heads):
        left, right = windows[head]
        result = acc[head, :, : right - left] / sum_ref[head][:, :1]
        result = result.astype(jnp.bfloat16)
        if head == 0:
            out_ref[:, left:right] = result
        else:
            shared = windows[head - 1][1]
            kept = jnp.where(
                member(head)[:, : shared - left], result[:, : shared - left], out_ref[:, left:shared]
            )
            out_ref[:, left:shared] = kept
            out_ref[:, shared:right] = result[:, shared - left :]


def attend_all(query, begin, end, first, side, own, pieces):
    length, width = query.shape
    heads = width // HA
    offsets = [(-1, 0, False, None), (-1, 0, True, None)]
    for place, (_, offset, parity) in enumerate(pieces):
        offsets.append((place, offset, False, parity))
        if offset < 0:
            offsets.append((place, offset, True, parity))
    low, high = begin[0], end[length - 1]
    near = jnp.stack([first, low, high, side]).astype(jnp.int32)
    spread = lambda a: jnp.broadcast_to(a[:, None], (length, 128)).astype(jnp.int32)
    vmem = pl.BlockSpec(memory_space=pltpu.VMEM)
    return pl.pallas_call(
        functools.partial(attend_kernel, tuple(offsets)),
        out_shape=jax.ShapeDtypeStruct((length, width), jnp.bfloat16),
        in_specs=[pl.BlockSpec(memory_space=pltpu.SMEM)]
        + [vmem] * (3 + 4 + len(pieces)),
        out_specs=vmem,
        scratch_shapes=[
            pltpu.VMEM((heads, length, 384), jnp.float32),
            pltpu.VMEM((heads, length, 128), jnp.float32),
            pltpu.VMEM((heads, length, 128), jnp.float32),
            pltpu.VMEM((heads, length, 384), jnp.bfloat16),
        ],
        compiler_params=pltpu.CompilerParams(vmem_limit_bytes=48 * 2**20),
        name="attend",
    )(near, query, spread(begin), spread(end), *own, *[piece[0] for piece in pieces])


def locate(lengths, index):
    ends = jnp.cumsum(lengths)
    starts = ends - lengths
    count = lengths.shape[0]
    segment = jnp.sum((index[:, None] >= ends[None, :]).astype(jnp.int32), axis=1)
    segment = jnp.minimum(segment, count - 1)
    onehot = segment[:, None] == jnp.arange(count, dtype=jnp.int32)[None, :]
    begin = jnp.sum(jnp.where(onehot, starts[None, :], 0), axis=1)
    valid = (index >= 0) & (index < ends[count - 1])
    return (segment, begin, valid, onehot)


def convolve(inputs, border, cache, weight, position, onehot):
    taps = weight.shape[0]
    length = inputs.shape[0]
    extended = jnp.concatenate([border, inputs], axis=0)
    picks = onehot.astype(jnp.bfloat16)
    cached_rows = [
        jnp.dot(picks, cache[:, slot, :], preferred_element_type=jnp.float32)
        for slot in range(taps - 1)
    ]
    result = weight[0][None, :] * inputs.astype(jnp.float32)
    for lag in range(1, taps):
        shifted = extended[taps - 1 - lag : taps - 1 - lag + length].astype(jnp.float32)
        slot_index = taps - 1 + position - lag
        fallback = jnp.zeros_like(shifted)
        for slot in range(taps - 1):
            fallback = jnp.where((slot_index == slot)[:, None], cached_rows[slot], fallback)
        shifted = jnp.where((position >= lag)[:, None], shifted, fallback)
        result = result + weight[lag][None, :] * shifted
    return jax.nn.silu(result).astype(jnp.bfloat16)


def per_device(
    residual,
    x_in,
    z_in,
    bc_in,
    dt_in,
    conv_x_weight,
    conv_bc_weight,
    conv_x_cache,
    conv_bc_cache,
    ssm_cache,
    dt_bias,
    a_log,
    d_skip,
    norm_gain,
    out_weight,
    attn_gain,
    q_weight,
    q_down,
    q_up,
    cache_keys,
    cache_values,
    new_keys,
    new_values,
    lengths,
):
    high_precision = lax.Precision.HIGH
    length = x_in.shape[0]
    taps = conv_x_weight.shape[0]
    seq_index = lax.axis_index("seq")
    seq_count = lax.axis_size("seq")
    reach = seq_count // 4 + 1
    first = seq_index * length
    packed = jnp.concatenate([cache_keys, cache_values, new_keys, new_values], axis=1)
    packed_cache = packed[:, : 2 * cache_keys.shape[1]]
    relay = reach == 3 and seq_count % 2 == 0
    if relay:
        pairs = range(0, seq_count, 2)
        halo = (
            lax.ppermute(packed, "seq", [(s, s + 1) for s in pairs]),
            lax.ppermute(packed_cache, "seq", [(s + 1, s) for s in pairs]),
            shifted_2(packed, "seq", 2),
            shifted_2(packed_cache, "seq", -2),
        )
    else:
        halo = None
        behind = [shifted_2(packed, "seq", distance) for distance in range(1, reach + 1)]
        forward = [shifted_2(packed_cache, "seq", -distance) for distance in range(1, reach + 1)]
    local_index = first + jnp.arange(length, dtype=jnp.int32)
    segment, begin, valid, onehot = locate(lengths, local_index)
    position = local_index - begin
    border = shifted_2(
        jnp.concatenate([x_in[length - taps + 1 :], bc_in[length - taps + 1 :]], axis=1), "seq", 1
    )
    x_border, bc_border = border[:, : x_in.shape[1]], border[:, x_in.shape[1] :]
    x_conv = convolve(x_in, x_border, conv_x_cache, conv_x_weight, position, onehot)
    bc_conv = convolve(bc_in, bc_border, conv_bc_cache, conv_bc_weight, position, onehot)
    heads = dt_bias.shape[0]
    state_size = bc_in.shape[1] // 2
    head_size = x_in.shape[1] // heads
    prompts = lengths.shape[0]
    values_bf = x_conv.reshape(length, heads, head_size)
    values = x_conv.astype(jnp.float32).reshape(length, heads, head_size)
    inputs_b = bc_conv[:, :state_size]
    inputs_c = bc_conv[:, state_size:]
    step = jax.nn.softplus(dt_in + dt_bias[None, :])
    log_decay = -step * jnp.exp(a_log)[None, :]
    cumulative = jnp.cumsum(log_decay, axis=0)
    local_begin = jnp.maximum(begin - first, 0)
    before = jnp.take(cumulative - log_decay, local_begin, axis=0)
    from_begin = jnp.exp(cumulative - before)
    block = min(length, 512)
    pair_scores = jnp.dot(inputs_c, inputs_b.T, preferred_element_type=jnp.float32)
    cumulative_t = cumulative.T
    step_t = step.T
    order = jnp.arange(length, dtype=jnp.int32)

    def intra(block_start):
        query_rows = block_start + jnp.arange(block, dtype=jnp.int32)
        same = (segment[:, None] == segment[None, :]) & (query_rows[:, None] >= order[None, :])
        gap = cumulative_t[:, :, None] - cumulative_t[:, None, :]
        factor = jnp.where(same[None], jnp.exp(jnp.where(same[None], gap, 0.0)), 0.0)
        weights = factor * step_t[:, None, :] * pair_scores[None, :, :]
        return jnp.einsum(
            "hqs,shd->qhd",
            weights,
            values_bf,
            precision=high_precision,
            preferred_element_type=jnp.float32,
        )

    intra_out = lax.map(intra, jnp.arange(length // block, dtype=jnp.int32) * block).reshape(
        length, heads, head_size
    )
    last_segment = segment[length - 1]
    in_last = segment == last_segment
    tail_weight = (
        jnp.where(in_last[:, None], jnp.exp(cumulative[length - 1][None, :] - cumulative), 0.0)
        * step
    )
    inner = heads * head_size
    spread = jnp.repeat(jnp.eye(heads, dtype=jnp.float32), head_size, axis=1)

    def widen(per_head):
        return jnp.dot(per_head, spread, precision=lax.Precision.HIGHEST)

    local_state = lax.dot_general(
        inputs_b.astype(jnp.float32),
        widen(tail_weight) * x_conv.astype(jnp.float32),
        (((0,), (0,)), ((), ())),
        precision=high_precision,
        preferred_element_type=jnp.float32,
    )
    whole_decay = jnp.exp(cumulative[length - 1] - before[length - 1])
    starts_here = begin[length - 1] >= first
    table = jnp.transpose(ssm_cache, (0, 3, 1, 2)).reshape(prompts, state_size, inner)
    cached_last = lax.dynamic_index_in_dim(table, last_segment, 0, keepdims=False)
    wide_decay = jnp.repeat(whole_decay, head_size)[None, :]
    chain_state = local_state + jnp.where(starts_here, wide_decay * cached_last, 0.0)
    chain_decay = jnp.where(starts_here, jnp.zeros_like(wide_decay), wide_decay)
    chain = jnp.concatenate(
        [chain_state, jnp.broadcast_to(chain_decay, (16, inner))], axis=0
    ).astype(jnp.bfloat16)
    continuing = position[0] > 0
    replace = (jnp.arange(prompts, dtype=jnp.int32) == segment[0]) & continuing
    taken = jnp.broadcast_to(
        jnp.repeat(replace.astype(jnp.float32), state_size)[:, None], (prompts * state_size, 128)
    )
    selected = (onehot[:, :, None].astype(jnp.bfloat16) * inputs_c[:, None, :]).reshape(
        length, prompts * state_size
    )
    parts = (
        chain,
        table.reshape(prompts * state_size, inner),
        taken,
        selected,
        widen(from_begin),
        intra_out.reshape(length, inner),
        x_conv,
        jnp.repeat(d_skip, head_size)[None, :],
        z_in,
        norm_gain[None, :],
    )
    hidden, query, *arrived = project(
        reach, parts, residual, attn_gain, q_up, out_weight, q_weight, q_down, halo
    )
    if relay:
        pieces = (
            (arrived[0], -1, 0),
            (halo[0], -1, 1),
            (halo[2], -2, None),
            (arrived[1], -3, None),
            (halo[1], 1, 0),
            (arrived[2], 1, 1),
            (halo[3], 2, None),
            (arrived[3], 3, None),
        )
    else:
        pieces = [(piece, -place - 1, None) for place, piece in enumerate(behind)]
        pieces += [(piece, place + 1, None) for place, piece in enumerate(forward)]
    ends = jnp.cumsum(lengths)
    finish = jnp.sum(jnp.where(onehot, ends[None, :], 0), axis=1)
    attended = attend_all(
        query,
        begin,
        finish,
        first,
        seq_index % 2,
        (cache_keys, cache_values, new_keys, new_values),
        pieces,
    )
    return (hidden, attended)


def solution(mesh):
    in_specs = (
        P(("seq", "tp"), None),
        P("seq", "tp"),
        P("seq", "tp"),
        P("seq", None),
        P("seq", "tp"),
        P(None, "tp"),
        P(),
        P(None, None, "tp"),
        P(),
        P(None, "tp", None, None),
        P("tp"),
        P("tp"),
        P("tp"),
        P("tp"),
        P("tp", None),
        P(),
        P(None, "tp"),
        P(),
        P(None, "tp"),
        P("seq", "tp"),
        P("seq", "tp"),
        P("seq", "tp"),
        P("seq", "tp"),
        P(),
    )
    out_specs = (P(("seq", "tp"), None), P("seq", "tp"))
    return jax.shard_map(
        per_device, mesh=mesh, in_specs=in_specs, out_specs=out_specs, check_vma=False
    )
```
